256 devices in a mesh: freq: 16 (over x, y_lo, core), rcv: 16 (over z, y_hi).
Axes of the slice: x: 4, y: 4 (y_hi: 2, y_lo: 2; y = y_hi * 2 + y_lo), z: 8, core: 2. Of those that a mesh axis runs over, the one named last changes fastest.
Arguments:
- reflection: bfloat16 [2, 32, 4096, 4096], P(None, 'freq', 'rcv'), may hold values from -1 to 1, as said below
- focus_plus: bfloat16 [2, 32, 128, 4096], P(None, 'freq', None, 'rcv'), may hold values from -6 to 6
- focus_direct: bfloat16 [2, 32, 128, 4096], P(None, 'freq', None, 'rcv'), may hold values from -6 to 6
- arrival: int32 [128, 4096], P(None, 'rcv'), may hold values from 2 to 31
Outputs:
- focus_minus: bfloat16 [2, 32, 128, 4096], P(None, 'freq', None, 'rcv')
- focus_next: bfloat16 [2, 32, 128, 4096], P(None, 'freq', None, 'rcv')
The draws below stay inside these ranges and needn't reach their ends.
Inputs may be any that keep to these rules, and one draw needn't show every extreme that they name: reflection is reciprocal: reflection[c, k, r, s] equals reflection[c, k, s, r] for all components, frequencies and positions.
All inputs are finite; a program needn't handle non-finite values.
Results may differ from the reference program's by a relative error of at most 0.0056.
Values may be sent and summed in bfloat16 or wider, within the bound.
A program may use at most 64 MiB of HBM per device.

```python
import math
import jax
import jax.numpy as jnp
from jax import lax

NR = 4096
P_SIZE = 128
NF = 32


def draw_reflection(key, part):
    key = jax.random.fold_in(key, 11)

    def one_bin(bin_index):
        bin_key = jax.random.fold_in(key, bin_index)
        entries = jax.random.normal(bin_key, (2, NR, NR), jnp.float32)
        return ((entries + jnp.swapaxes(entries, 1, 2)) * (0.5 / math.sqrt(NR))).astype(jnp.bfloat16)
    return jnp.moveaxis(lax.map(one_bin, jnp.arange(NF, dtype=jnp.int32)), 0, 1)


def place_ends(drawn, key, least, high):
    dims = drawn.shape
    spot = [jax.random.randint(jax.random.fold_in(key, axis), (), 0, dims[axis]) for axis in range(len(dims))]
    drawn = drawn.at[tuple(spot)].set(least)
    longest = dims.index(max(dims))
    spot[longest] = (spot[longest] + 1) % dims[longest]
    return drawn.at[tuple(spot)].set(high)


def shard_levels(stream_key, dims, split, least, largest):
    factor_of = 1.0
    for dim, blocks in split:
        heights = jax.random.uniform(jax.random.fold_in(jax.random.fold_in(stream_key, 6), dim), (blocks,), jnp.float32, least / len(split), largest / len(split))
        factor_of = factor_of * jnp.repeat(jnp.exp(heights), dims[dim] // blocks).reshape((-1,) + (1,) * (len(dims) - 1 - dim))
    return factor_of


def centred(stream_key, extent, scale, reach, shards=(), kind=jnp.bfloat16):
    values = jax.random.normal(stream_key, extent, jnp.float32) * scale
    if len(shards) > 0:
        values = shard_levels(stream_key, extent, shards, -0.22, 0.18) * values
    return jnp.clip(values, min=-reach, max=reach).astype(kind)


def setup_inputs(seed: int = 0) -> dict:
    seeds = jax.random.split(jax.random.key(seed), 5)
    reflection = draw_reflection(jax.random.fold_in(seeds[4], 71), 0)
    focus_plus = centred(seeds[1], (2, NF, P_SIZE, NR), 1.0, 6.0, ((1, 16), (3, 16)))
    focus_direct = centred(seeds[2], (2, NF, P_SIZE, NR), 1.0, 6.0, ((1, 16), (3, 16)))
    arrival = place_ends(jax.random.randint(seeds[3], (P_SIZE, NR), max(1, NF // 12), NF), jax.random.fold_in(seeds[3], 1), max(1, NF // 12), NF - 1).astype(jnp.int32)
    return dict(reflection=reflection, focus_plus=focus_plus, focus_direct=focus_direct, arrival=arrival)


highest = lax.Precision.HIGHEST


def tables(freq_count, time_count):
    frequency = jnp.arange(freq_count, dtype=jnp.int32)
    sample = jnp.arange(time_count, dtype=jnp.int32)
    phase = (sample[:, None] * frequency[None, :]) % time_count
    angle = phase.astype(jnp.float32) * (2.0 * jnp.pi / time_count)
    return jnp.cos(angle), jnp.sin(angle)


def windowed(spectrum, arrival):
    freq_count = spectrum.shape[1]
    time_count = 2 * freq_count
    cosine_table, sine_table = tables(freq_count, time_count)
    real_part = spectrum[0].astype(jnp.float32).reshape(freq_count, -1)
    imag_part = spectrum[1].astype(jnp.float32).reshape(freq_count, -1)
    traces = (jnp.dot(cosine_table, real_part, precision=highest) - jnp.dot(sine_table, imag_part, precision=highest)) / freq_count
    traces = traces.reshape((time_count,) + spectrum.shape[2:])
    sample = jnp.arange(time_count, dtype=jnp.int32)[:, None, None]
    inside = (sample < arrival[None]) | (sample > time_count - arrival[None])
    masked = jnp.where(inside, traces, jnp.float32(0.0)).reshape(time_count, -1)
    back_real = jnp.dot(cosine_table.T, masked, precision=highest)
    back_imag = -jnp.dot(sine_table.T, masked, precision=highest)
    return jnp.stack([back_real, back_imag]).reshape(spectrum.shape).astype(jnp.bfloat16)


def reference(reflection, focus_plus, focus_direct, arrival):
    frequency = jnp.arange(reflection.shape[1], dtype=jnp.int32)

    def up_bin(bin_index):
        slab = lax.dynamic_index_in_dim(reflection, bin_index, 1, keepdims=False)
        focusing = lax.dynamic_index_in_dim(focus_plus, bin_index, 1, keepdims=False)
        real_part = jnp.dot(focusing[0], slab[0].T, preferred_element_type=jnp.float32) - jnp.dot(focusing[1], slab[1].T, preferred_element_type=jnp.float32)
        imag_part = jnp.dot(focusing[1], slab[0].T, preferred_element_type=jnp.float32) + jnp.dot(focusing[0], slab[1].T, preferred_element_type=jnp.float32)
        return jnp.stack([real_part, imag_part]).astype(jnp.bfloat16)

    upgoing = jnp.moveaxis(lax.map(up_bin, frequency), 0, 1)
    focus_minus = windowed(upgoing, arrival)

    def down_bin(bin_index):
        slab = lax.dynamic_index_in_dim(reflection, bin_index, 1, keepdims=False)
        focusing = lax.dynamic_index_in_dim(focus_minus, bin_index, 1, keepdims=False)
        real_part = jnp.dot(focusing[0], slab[0], preferred_element_type=jnp.float32) + jnp.dot(focusing[1], slab[1], preferred_element_type=jnp.float32)
        imag_part = jnp.dot(focusing[1], slab[0], preferred_element_type=jnp.float32) - jnp.dot(focusing[0], slab[1], preferred_element_type=jnp.float32)
        return jnp.stack([real_part, imag_part]).astype(jnp.bfloat16)

    downgoing = jnp.moveaxis(lax.map(down_bin, frequency), 0, 1)
    correction = windowed(downgoing, arrival)
    focus_next = (focus_direct.astype(jnp.float32) + correction.astype(jnp.float32)).astype(jnp.bfloat16)
    return (focus_minus, focus_next)
```

```python
import functools

import jax
import jax.numpy as jnp
import ml_dtypes
import numpy as np
from jax import lax
from jax.experimental import pallas as pl
from jax.experimental.pallas import tpu as pltpu
from jax.sharding import PartitionSpec as P

MESH = pl.DeviceIdType.MESH
BF = jnp.bfloat16
F32 = jnp.float32

FOCAL = 128
BLOCK = 256
POSITIONS = 4096
GROUP = 16
RING = 8
SAMPLES = 64
CHUNKS = 2
PC = FOCAL // CHUNKS
PG = PC // 8
NH = GROUP // PG
W = BLOCK // NH
ROWS = 8 * SAMPLES

ARRIVALS = (
    ((0, 1), "f"),
    ((0, -1), "by"),
    ((1, 0), "f"),
    ((0, 2), "fy"),
    ((0, -2), "by"),
    ((1, -1), ""),
    ((1, 1), ""),
    ((0, 3), "f"),
    ((0, -3), ""),
    ((1, 2), "f"),
    ((1, -2), "b"),
    ((0, 4), "y"),
    ((1, 3), ""),
    ((1, -3), ""),
    ((1, 4), ""),
)
SLOT = {where: number for number, (where, _) in enumerate(ARRIVALS)}


def after(where, send):
    column, distance = where
    if send == "y":
        return (1 - column, distance)
    return (column, distance + (1 if send == "f" else -1))


def split(table):
    high = table.astype(ml_dtypes.bfloat16)
    low = (table - high.astype(np.float64)).astype(ml_dtypes.bfloat16)
    return np.stack([high, low])


def transforms():
    sample = np.arange(SAMPLES)
    frequency = np.arange(SAMPLES // 2)
    angle = 2.0 * np.pi * ((sample[:, None] * frequency[None, :]) % SAMPLES) / SAMPLES
    table = np.stack([np.cos(angle), -np.sin(angle)], 1).reshape(SAMPLES, 2, GROUP, 2).transpose(0, 2, 1, 3)
    table = table.reshape(SAMPLES, SAMPLES)
    eye = np.eye(8)
    forth = np.kron(table / (SAMPLES // 2), eye)
    back = np.kron(table.T, eye)
    return split(forth), split(back)


def dot(left, right):
    return lax.dot_general(left, right, (((1,), (0,)), ((), ())), preferred_element_type=F32)


def dot_t(left, right):
    return lax.dot_general(left, right, (((1,), (1,)), ((), ())), preferred_element_type=F32)


def kernel(
    refl_hbm, plus_hbm, direct_hbm, arrival_hbm, forth_hbm, back_hbm,
    minus_hbm, next_hbm,
    refl, direct, arrival, forth, back, gathered, send_up, got_up, send_back, got_back, masked, result,
    load_sems, plus_sems, out_sems, gather_recv, gather_send, swap_recv, swap_send,
):
    me_f = lax.axis_index("freq")
    me_r = lax.axis_index("rcv")
    core = lax.rem(me_f, 2)
    z = lax.div(me_r, 2)
    high = lax.rem(me_r, 2)
    turn = 1 - 2 * core

    def place(column, distance):
        ring = lax.rem(z - turn * distance + 2 * RING, RING)
        return ring * 2 + (high if column == 0 else 1 - high)

    targets = {
        "f": (me_f, place(0, -1)),
        "b": (me_f, place(0, 1)),
        "y": (me_f, place(1, 0)),
    }

    loads = [
        pltpu.make_async_copy(source, target, load_sems.at[number])
        for number, (source, target) in enumerate(
            ((refl_hbm, refl), (direct_hbm, direct), (arrival_hbm, arrival), (forth_hbm, forth), (back_hbm, back))
        )
    ]

    def block_of(job, where):
        start = pl.multiple_of(place(*where) * BLOCK, BLOCK)
        return gathered.at[job, :, :, :, pl.ds(start, BLOCK)]

    own = [
        pltpu.make_async_copy(
            plus_hbm.at[:, :, pl.ds(chunk * PC, PC), :], block_of(chunk, (0, 0)), plus_sems.at[chunk]
        )
        for chunk in range(CHUNKS)
    ]
    for copy in own:
        copy.start()
    for copy in loads:
        copy.start()

    barrier = pltpu.get_barrier_semaphore()
    for target in targets.values():
        pl.semaphore_signal(barrier, inc=1, device_id=target, device_id_type=MESH)

    @pl.loop(1, GROUP)
    def _(step):
        pl.semaphore_signal(
            barrier, inc=1, device_id=(lax.rem(me_f + step, GROUP), me_r), device_id_type=MESH
        )

    pl.semaphore_wait(barrier, 3 + GROUP - 1)

    def gather_copy(job, where, send):
        block = block_of(job, where)
        return pltpu.make_async_remote_copy(
            src_ref=block,
            dst_ref=block,
            send_sem=gather_send.at[job],
            recv_sem=gather_recv.at[job, SLOT[after(where, send)]],
            device_id=targets[send],
            device_id_type=MESH,
        )

    def gather_start(job):
        for send in "fby":
            gather_copy(job, (0, 0), send).start()

    def gather_step(job, number):
        where, sends = ARRIVALS[number]
        block = block_of(job, where)
        pltpu.make_async_remote_copy(
            src_ref=block,
            dst_ref=block,
            send_sem=gather_send.at[job],
            recv_sem=gather_recv.at[job, number],
            device_id=targets["f"],
            device_id_type=MESH,
        ).wait_recv()
        for send in sends:
            gather_copy(job, where, send).start()

    def gather_end(job):
        sent = gathered.at[job, :, :, :, pl.ds(0, (GROUP - 1) * BLOCK)]
        pltpu.make_async_remote_copy(
            src_ref=sent,
            dst_ref=sent,
            send_sem=gather_send.at[job],
            recv_sem=gather_recv.at[job, 0],
            device_id=targets["f"],
            device_id_type=MESH,
        ).wait_send()

    def products(job):
        sums = []
        for freq in range(2):
            left = gathered[job, :, freq].reshape(2 * PC, POSITIONS)
            with_real = dot_t(left, refl[0, freq])
            with_imag = dot_t(left, refl[1, freq])
            if job < CHUNKS:
                sums.append((with_real[:PC] - with_imag[PC:], with_real[PC:] + with_imag[:PC]))
            else:
                sums.append((with_real[:PC] + with_imag[PC:], with_real[PC:] - with_imag[:PC]))
        for comp in range(2):
            pair = [sums[freq][comp].reshape(PG, 8, BLOCK) for freq in range(2)]
            pair = jnp.concatenate(pair, axis=1).astype(BF)
            for part in range(NH):
                send_up[job, pl.ds(part * PG, PG), pl.ds(comp * 16, 16), :] = pair[:, :, part * W:(part + 1) * W]

    def swap_copy(job, way, sent, got, owner, count=1):
        if count == 1:
            source, target = sent.at[job, owner], got.at[job, me_f]
        else:
            source, target = sent.at[job, pl.ds(0, count)], got.at[job, pl.ds(0, count)]
        return pltpu.make_async_remote_copy(
            src_ref=source,
            dst_ref=target,
            send_sem=swap_send.at[job, way],
            recv_sem=swap_recv.at[job, way],
            device_id=(owner, me_r),
            device_id_type=MESH,
        )

    def swap_start(job, way, sent, got):
        @pl.loop(1, GROUP)
        def _(step):
            swap_copy(job, way, sent, got, lax.rem(me_f + step, GROUP)).start()

        got[job, me_f] = sent[job, me_f]

    def swap_wait(job, way, sent, got):
        other = lax.rem(me_f + 1, GROUP)
        swap_copy(job, way, sent, got, other, GROUP - 1).wait_recv()

    def swap_end(job, way, sent, got):
        other = lax.rem(me_f + 1, GROUP)
        swap_copy(job, way, sent, got, other, GROUP - 1).wait_send()

    def window(job):
        chunk = job % CHUNKS
        first = pl.multiple_of(chunk * PC + lax.rem(me_f, PG) * 8, 8)
        column = pl.multiple_of(lax.div(me_f, PG) * W, W)
        times = arrival[pl.ds(first, 8), pl.ds(column, W)][None]
        spectra = got_up[job].reshape(ROWS, W)
        for part in range(4):
            rows = ROWS // 4
            here = pl.ds(part * rows, rows)
            traces = dot(forth[0, here], spectra) + dot(forth[1, here], spectra)
            sample = lax.broadcasted_iota(jnp.int32, (rows // 8, 8, W), 0) + part * (rows // 8)
            inside = (sample < times) | (sample > SAMPLES - times)
            kept = jnp.where(inside, traces.reshape(rows // 8, 8, W), 0.0).reshape(rows, W)
            upper = kept.astype(BF)
            masked[0, here] = upper
            masked[1, here] = (kept - upper.astype(F32)).astype(BF)
        for part in range(4):
            here = pl.ds(part * rows, rows)
            spectrum = dot(back[0, here], masked[0]) + dot(back[1, here], masked[0]) + dot(back[0, here], masked[1])
            send_back[job, pl.ds(part * 4, 4)] = spectrum.astype(BF).reshape(4, 32, W)

    def returned(job, comp):
        value = got_back[job, :, pl.ds(comp * 16, 16), :].astype(F32)
        parts = []
        for freq in range(2):
            one = value[:, freq * 8:(freq + 1) * 8, :].reshape(NH, PC, W)
            parts.append(jnp.concatenate([one[part] for part in range(NH)], axis=1))
        return parts

    def place_minus(job):
        chunk = job % CHUNKS
        start = pl.multiple_of(me_r * BLOCK, BLOCK)
        for comp in range(2):
            for freq, value in enumerate(returned(job, comp)):
                gathered[CHUNKS + chunk, comp, freq, :, pl.ds(start, BLOCK)] = value.astype(BF)
        minus_copy(chunk).start()

    def minus_copy(chunk):
        return pltpu.make_async_copy(
            block_of(CHUNKS + chunk, (0, 0)), minus_hbm.at[:, :, pl.ds(chunk * PC, PC), :], out_sems.at[chunk]
        )

    def next_copy(chunk):
        here = pl.ds(chunk * PC, PC)
        return pltpu.make_async_copy(
            result.at[:, :, here, :], next_hbm.at[:, :, here, :], out_sems.at[CHUNKS + chunk]
        )

    def place_next(job):
        chunk = job % CHUNKS
        here = pl.ds(chunk * PC, PC)
        for comp in range(2):
            for freq, value in enumerate(returned(job, comp)):
                value = value.astype(BF).astype(F32)
                result[comp, freq, here, :] = (direct[comp, freq, here, :].astype(F32) + value).astype(BF)
        next_copy(chunk).start()

    steps = []

    def plan(job, begin):
        for number in range(len(ARRIVALS)):
            when = begin + STEP_TIMES[number]
            steps.append((when, functools.partial(gather_step, job, number)))

    STEP_TIMES = (3.5, 3.6, 3.7, 7.0, 7.1, 7.2, 7.3, 10.5, 10.6, 10.7, 10.8, 13.0, 13.5, 13.6, 15.0)

    def tail(job, begin):
        steps.append((begin, functools.partial(products, job)))
        steps.append((begin + 2.0, functools.partial(swap_start, job, 0, send_up, got_up)))
        steps.append((begin + 6.5, functools.partial(swap_wait, job, 0, send_up, got_up)))
        steps.append((begin + 6.6, functools.partial(window, job)))
        steps.append((begin + 8.0, functools.partial(swap_start, job, 1, send_back, got_back)))
        steps.append((begin + 12.0, functools.partial(swap_wait, job, 1, send_back, got_back)))
        steps.append((begin + 12.1, functools.partial(place_minus if job < CHUNKS else place_next, job)))

    def first_products():
        loads[0].wait()

    def first_window():
        for copy in loads[2:]:
            copy.wait()

    START = (0.0, 7.0, 29.0, 42.0) if CHUNKS == 2 else (0.0, 40.0)
    LENGTH = 16.0
    for job in range(2 * CHUNKS):
        begin = START[job]
        if job < CHUNKS:
            steps.append((begin - 0.1, own[job].wait))
        steps.append((begin, functools.partial(gather_start, job)))
        plan(job, begin)
        end = begin + LENGTH + (5.0 if job == 1 else 0.0)
        if job == 0:
            steps.append((end - 0.1, first_products))
            steps.append((end + 6.55, first_window))
        if job == CHUNKS:
            steps.append((end - 0.1, loads[1].wait))
        tail(job, end)
    for _, step in sorted(steps, key=lambda entry: entry[0]):
        step()

    for job in range(2 * CHUNKS):
        gather_end(job)
        swap_end(job, 0, send_up, got_up)
        swap_end(job, 1, send_back, got_back)
    for chunk in range(CHUNKS):
        minus_copy(chunk).wait()
        next_copy(chunk).wait()


def local(reflection, focus_plus, focus_direct, arrival):
    forth, back = transforms()
    jobs = 2 * CHUNKS
    swap = (jobs, GROUP, 32, W)
    anywhere = pl.BlockSpec(memory_space=pl.ANY)
    output = jax.ShapeDtypeStruct(focus_plus.shape, BF)
    return pl.pallas_call(
        kernel,
        out_shape=(output, output),
        in_specs=[anywhere] * 6,
        out_specs=(anywhere, anywhere),
        scratch_shapes=[
            pltpu.VMEM(reflection.shape, BF),
            pltpu.VMEM(focus_direct.shape, BF),
            pltpu.VMEM(arrival.shape, jnp.int32),
            pltpu.VMEM(forth.shape, BF),
            pltpu.VMEM(back.shape, BF),
            pltpu.VMEM((jobs, 2, 2, PC, POSITIONS), BF),
            pltpu.VMEM(swap, BF),
            pltpu.VMEM(swap, BF),
            pltpu.VMEM(swap, BF),
            pltpu.VMEM(swap, BF),
            pltpu.VMEM((2, ROWS, W), BF),
            pltpu.VMEM(focus_direct.shape, BF),
            pltpu.SemaphoreType.DMA((5,)),
            pltpu.SemaphoreType.DMA((CHUNKS,)),
            pltpu.SemaphoreType.DMA((2 * CHUNKS,)),
            pltpu.SemaphoreType.DMA((jobs, len(ARRIVALS))),
            pltpu.SemaphoreType.DMA((jobs,)),
            pltpu.SemaphoreType.DMA((jobs, 2)),
            pltpu.SemaphoreType.DMA((jobs, 2)),
        ],
        compiler_params=pltpu.CompilerParams(
            collective_id=0, has_side_effects=True, vmem_limit_bytes=48 * 2**20
        ),
    )(reflection, focus_plus, focus_direct, arrival, jnp.asarray(forth), jnp.asarray(back))


def solution(mesh):
    return jax.shard_map(
        local,
        mesh=mesh,
        in_specs=(
            P(None, "freq", "rcv", None),
            P(None, "freq", None, "rcv"),
            P(None, "freq", None, "rcv"),
            P(None, "rcv"),
        ),
        out_specs=(P(None, "freq", None, "rcv"), P(None, "freq", None, "rcv")),
        check_vma=False,
    )
```

```python
import functools

import jax
import jax.numpy as jnp
import ml_dtypes
import numpy as np
from jax import lax
from jax.experimental import pallas as pl
from jax.experimental.pallas import tpu as pltpu
from jax.sharding import PartitionSpec as P

MESH = pl.DeviceIdType.MESH
BF = jnp.bfloat16
F32 = jnp.float32

FOCAL = 128
BLOCK = 256
GROUP = 16
FAR_FIRST = sorted(range(1, GROUP), key=lambda step: -min(step, GROUP - step))
RING = 8
SAMPLES = 64
CHUNKS = 2
PC = FOCAL // CHUNKS
PG = PC // 8
NH = GROUP // PG
W = BLOCK // NH
BEGIN = (0.0, 2.3, 32.5, 34.8)
ROWS = 8 * SAMPLES

ARRIVALS = (
    ((0, 1), "fy", 3.0),
    ((0, -1), "by", 3.4),
    ((1, 0), "", 3.6),
    ((0, -2), "by", 7.6),
    ((0, 2), "f", 8.2),
    ((1, 1), "f", 10.4),
    ((1, -1), "", 11.0),
    ((0, -3), "", 12.0),
    ((0, 3), "f", 12.7),
    ((1, 2), "f", 15.6),
    ((0, 4), "y", 17.0),
    ((1, -2), "b", 17.6),
    ((1, 3), "", 19.6),
    ((1, 4), "", 22.3),
    ((1, -3), "", 22.5),
)
END = 22.7
SLOT = {where: number for number, (where, _, _) in enumerate(ARRIVALS)}


def after(where, send):
    column, distance = where
    if send == "y":
        return (1 - column, distance)
    return (column, distance + (1 if send == "f" else -1))


def split(table):
    high = table.astype(ml_dtypes.bfloat16)
    low = (table - high.astype(np.float64)).astype(ml_dtypes.bfloat16)
    return np.stack([high, low])


def transforms():
    sample = np.arange(SAMPLES)
    frequency = np.arange(SAMPLES // 2)
    angle = 2.0 * np.pi * ((sample[:, None] * frequency[None, :]) % SAMPLES) / SAMPLES
    table = np.stack([np.cos(angle), -np.sin(angle)], 1).reshape(SAMPLES, 2, GROUP, 2).transpose(0, 2, 3, 1)
    table = table.reshape(SAMPLES, SAMPLES)
    eye = np.eye(8)
    forth = np.kron(table / (SAMPLES // 2), eye)
    back = np.kron(table.T, eye)
    return split(forth), split(back)


def dot(left, right):
    return lax.dot_general(left, right, (((1,), (0,)), ((), ())), preferred_element_type=F32)


def dot_t(left, right):
    return lax.dot_general(left, right, (((1,), (1,)), ((), ())), preferred_element_type=F32)


def kernel(
    refl_hbm, plus_hbm, direct_hbm, arrival_hbm, forth_hbm, back_hbm,
    minus_hbm, next_hbm,
    refl, direct, arrival, forth, back, gathered, send_up, got_up, send_back, got_back, masked, result, sums,
    load_sems, plus_sems, out_sems, gather_recv, gather_send, swap_recv, swap_send,
):
    me_f = lax.axis_index("freq")
    me_r = lax.axis_index("rcv")
    core = lax.rem(me_f, 2)
    z = lax.div(me_r, 2)
    high = lax.rem(me_r, 2)
    turn = 1 - 2 * core

    def place(column, distance):
        ring = lax.rem(z - turn * distance + 2 * RING, RING)
        return ring * 2 + (high if column == 0 else 1 - high)

    targets = {
        "f": (me_f, place(0, -1)),
        "b": (me_f, place(0, 1)),
        "y": (me_f, place(1, 0)),
    }

    loads = [
        pltpu.make_async_copy(source, target, load_sems.at[number])
        for number, (source, target) in enumerate(
            ((refl_hbm, refl), (direct_hbm, direct), (arrival_hbm, arrival), (forth_hbm, forth), (back_hbm, back))
        )
    ]

    def block_of(job, where):
        return gathered.at[job, place(*where)]

    own = [
        pltpu.make_async_copy(
            plus_hbm.at[:, :, pl.ds(chunk * PC, PC), :], block_of(chunk, (0, 0)), plus_sems.at[chunk]
        )
        for chunk in range(CHUNKS)
    ]
    for copy in own:
        copy.start()
    for copy in loads:
        copy.start()

    barrier = pltpu.get_barrier_semaphore()
    for target in targets.values():
        pl.semaphore_signal(barrier, inc=1, device_id=target, device_id_type=MESH)

    @pl.loop(1, GROUP)
    def _(step):
        pl.semaphore_signal(
            barrier, inc=1, device_id=(lax.rem(me_f + step, GROUP), me_r), device_id_type=MESH
        )

    pl.semaphore_wait(barrier, 3 + GROUP - 1)

    def gather_copy(job, where, send):
        block = block_of(job, where)
        return pltpu.make_async_remote_copy(
            src_ref=block,
            dst_ref=block,
            send_sem=gather_send.at[job],
            recv_sem=gather_recv.at[job, SLOT[after(where, send)]],
            device_id=targets[send],
            device_id_type=MESH,
        )

    def gather_start(job):
        for send in "fby":
            gather_copy(job, (0, 0), send).start()

    def gather_step(job, number):
        where, sends, _ = ARRIVALS[number]
        block = block_of(job, where)
        pltpu.make_async_remote_copy(
            src_ref=block,
            dst_ref=block,
            send_sem=gather_send.at[job],
            recv_sem=gather_recv.at[job, number],
            device_id=targets["f"],
            device_id_type=MESH,
        ).wait_recv()
        for send in sends:
            gather_copy(job, where, send).start()

    def gather_end(job):
        sent = gathered.at[job, pl.ds(0, GROUP - 1)]
        pltpu.make_async_remote_copy(
            src_ref=sent,
            dst_ref=sent,
            send_sem=gather_send.at[job],
            recv_sem=gather_recv.at[job, 0],
            device_id=targets["f"],
            device_id_type=MESH,
        ).wait_send()

    def accumulate(job, where):
        owner = place(*where)
        here = pl.ds(pl.multiple_of(owner * BLOCK, BLOCK), BLOCK)
        for freq in range(2):
            left = gathered[job, owner, :, freq].reshape(2 * PC, BLOCK)
            for comp in range(2):
                term = dot_t(left, refl[comp, freq, :, here])
                if where == (0, 0):
                    sums[job % CHUNKS, freq, comp] = term
                else:
                    sums[job % CHUNKS, freq, comp] += term

    def products(job):
        for freq in range(2):
            with_real = sums[job % CHUNKS, freq, 0]
            with_imag = sums[job % CHUNKS, freq, 1]
            if job < CHUNKS:
                both = (with_real[:PC] - with_imag[PC:], with_real[PC:] + with_imag[:PC])
            else:
                both = (with_real[:PC] + with_imag[PC:], with_real[PC:] - with_imag[:PC])
            pair = jnp.concatenate([one.reshape(PG, 8, BLOCK) for one in both], axis=1).astype(BF)
            for half in range(NH):
                send_up[job, pl.ds(half * PG, PG), pl.ds(freq * 16, 16), :] = pair[:, :, half * W:(half + 1) * W]

    def swap_copy(job, way, sent, got, owner, count=1):
        if count == 1:
            source, target = sent.at[job, owner], got.at[job, me_f]
        else:
            source, target = sent.at[job, pl.ds(0, count)], got.at[job, pl.ds(0, count)]
        return pltpu.make_async_remote_copy(
            src_ref=source,
            dst_ref=target,
            send_sem=swap_send.at[job, way],
            recv_sem=swap_recv.at[job, way],
            device_id=(owner, me_r),
            device_id_type=MESH,
        )

    def swap_start(job, way, sent, got):
        for step in FAR_FIRST:
            swap_copy(job, way, sent, got, lax.rem(me_f + step, GROUP)).start()

        got[job, me_f] = sent[job, me_f]

    def swap_wait(job, way, sent, got):
        other = lax.rem(me_f + 1, GROUP)
        swap_copy(job, way, sent, got, other, GROUP - 1).wait_recv()

    def swap_end(job, way, sent, got):
        other = lax.rem(me_f + 1, GROUP)
        swap_copy(job, way, sent, got, other, GROUP - 1).wait_send()

    def window(job):
        chunk = job % CHUNKS
        first = pl.multiple_of(chunk * PC + lax.rem(me_f, PG) * 8, 8)
        column = pl.multiple_of(lax.div(me_f, PG) * W, W)
        times = arrival[pl.ds(first, 8), pl.ds(column, W)][None]
        spectra = got_up[job].reshape(ROWS, W)
        for part in range(4):
            rows = ROWS // 4
            here = pl.ds(part * rows, rows)
            traces = dot(forth[0, here], spectra) + dot(forth[1, here], spectra)
            sample = lax.broadcasted_iota(jnp.int32, (rows // 8, 8, W), 0) + part * (rows // 8)
            inside = (sample < times) | (sample > SAMPLES - times)
            kept = jnp.where(inside, traces.reshape(rows // 8, 8, W), 0.0).reshape(rows, W)
            upper = kept.astype(BF)
            masked[0, here] = upper
            masked[1, here] = (kept - upper.astype(F32)).astype(BF)
        for part in range(4):
            here = pl.ds(part * rows, rows)
            spectrum = dot(back[0, here], masked[0]) + dot(back[1, here], masked[0]) + dot(back[0, here], masked[1])
            send_back[job, pl.ds(part * 4, 4)] = spectrum.astype(BF).reshape(4, 32, W)

    def returned(job):
        for freq in range(2):
            value = got_back[job, :, pl.ds(freq * 16, 16), :].astype(F32)
            for comp in range(2):
                one = value[:, comp * 8:(comp + 1) * 8, :].reshape(NH, PC, W)
                yield comp, freq, jnp.concatenate([one[half] for half in range(NH)], axis=1)

    def place_minus(job):
        chunk = job % CHUNKS
        for comp, freq, value in returned(job):
            gathered[CHUNKS + chunk, me_r, comp, freq] = value.astype(BF)
        minus_copy(chunk).start()

    def minus_copy(chunk):
        return pltpu.make_async_copy(
            block_of(CHUNKS + chunk, (0, 0)), minus_hbm.at[:, :, pl.ds(chunk * PC, PC), :], out_sems.at[chunk]
        )

    def next_copy(chunk):
        here = pl.ds(chunk * PC, PC)
        return pltpu.make_async_copy(
            result.at[:, :, here, :], next_hbm.at[:, :, here, :], out_sems.at[CHUNKS + chunk]
        )

    def place_next(job):
        chunk = job % CHUNKS
        here = pl.ds(chunk * PC, PC)
        for comp, freq, value in returned(job):
            value = value.astype(BF).astype(F32)
            result[comp, freq, here, :] = (direct[comp, freq, here, :].astype(F32) + value).astype(BF)
        next_copy(chunk).start()

    steps = []

    def plan(when, what, *given):
        steps.append((when, functools.partial(what, *given)))

    def wait_all(*copies):
        for copy in copies:
            copy.wait()

    for job, begin in enumerate(BEGIN):
        if job < CHUNKS:
            plan(begin - 0.01, wait_all, own[job])
        plan(begin, gather_start, job)
        if job == 0:
            plan(begin + 0.5, wait_all, loads[0])
        plan(begin + 0.6, accumulate, job, (0, 0))
        for number, (where, _, due) in enumerate(ARRIVALS):
            plan(begin + due, gather_step, job, number)
            plan(begin + due + 0.05, accumulate, job, where)
        end = begin + END
        if job == 0:
            plan(end + 4.0, wait_all, *loads[2:])
        if job == CHUNKS:
            plan(end, wait_all, loads[1])
        plan(end, products, job)
        plan(end + 0.1, swap_start, job, 0, send_up, got_up)
        plan(end + 4.0, swap_wait, job, 0, send_up, got_up)
        plan(end + 4.1, window, job)
        plan(end + 4.2, swap_start, job, 1, send_back, got_back)
        plan(end + 8.5, swap_wait, job, 1, send_back, got_back)
        plan(end + 8.6, place_minus if job < CHUNKS else place_next, job)
    for _, step in sorted(steps, key=lambda entry: entry[0]):
        step()

    for job in range(2 * CHUNKS):
        gather_end(job)
        swap_end(job, 0, send_up, got_up)
        swap_end(job, 1, send_back, got_back)
    for chunk in range(CHUNKS):
        minus_copy(chunk).wait()
        next_copy(chunk).wait()


def hand_on(minus, following, minus_out, next_out):
    minus_out[...] = minus[...]
    next_out[...] = following[...]


def local(reflection, focus_plus, focus_direct, arrival):
    forth, back = transforms()
    jobs = 2 * CHUNKS
    swap = (jobs, GROUP, 32, W)
    anywhere = pl.BlockSpec(memory_space=pl.ANY)
    output = jax.ShapeDtypeStruct(focus_plus.shape, BF)
    minus, following = pl.pallas_call(
        kernel,
        out_shape=(output, output),
        in_specs=[anywhere] * 6,
        out_specs=(anywhere, anywhere),
        scratch_shapes=[
            pltpu.VMEM(reflection.shape, BF),
            pltpu.VMEM(focus_direct.shape, BF),
            pltpu.VMEM(arrival.shape, jnp.int32),
            pltpu.VMEM(forth.shape, BF),
            pltpu.VMEM(back.shape, BF),
            pltpu.VMEM((jobs, GROUP, 2, 2, PC, BLOCK), BF),
            pltpu.VMEM(swap, BF),
            pltpu.VMEM(swap, BF),
            pltpu.VMEM(swap, BF),
            pltpu.VMEM(swap, BF),
            pltpu.VMEM((2, ROWS, W), BF),
            pltpu.VMEM(focus_direct.shape, BF),
            pltpu.VMEM((CHUNKS, 2, 2, 2 * PC, BLOCK), F32),
            pltpu.SemaphoreType.DMA((5,)),
            pltpu.SemaphoreType.DMA((CHUNKS,)),
            pltpu.SemaphoreType.DMA((2 * CHUNKS,)),
            pltpu.SemaphoreType.DMA((jobs, len(ARRIVALS))),
            pltpu.SemaphoreType.DMA((jobs,)),
            pltpu.SemaphoreType.DMA((jobs, 2)),
            pltpu.SemaphoreType.DMA((jobs, 2)),
        ],
        compiler_params=pltpu.CompilerParams(
            collective_id=0, has_side_effects=True, vmem_limit_bytes=62 * 2**20
        ),
    )(reflection, focus_plus, focus_direct, arrival, jnp.asarray(forth), jnp.asarray(back))
    return pl.pallas_call(
        hand_on,
        out_shape=(output, output),
        in_specs=[pl.BlockSpec(memory_space=pltpu.VMEM)] * 2,
        out_specs=(pl.BlockSpec(memory_space=pltpu.VMEM),) * 2,
    )(minus, following)


def solution(mesh):
    return jax.shard_map(
        local,
        mesh=mesh,
        in_specs=(
            P(None, "freq", "rcv", None),
            P(None, "freq", None, "rcv"),
            P(None, "freq", None, "rcv"),
            P(None, "rcv"),
        ),
        out_specs=(P(None, "freq", None, "rcv"), P(None, "freq", None, "rcv")),
        check_vma=False,
    )
```

```python
import functools

import jax
import jax.numpy as jnp
import ml_dtypes
import numpy as np
from jax import lax
from jax.experimental import pallas as pl
from jax.experimental.pallas import tpu as pltpu
from jax.sharding import PartitionSpec as P

MESH = pl.DeviceIdType.MESH
BF = jnp.bfloat16
F32 = jnp.float32

FOCAL = 128
BLOCK = 256
GROUP = 16
FAR_FIRST = sorted(range(1, GROUP), key=lambda step: -min(step, GROUP - step))
RING = 8
SAMPLES = 64
CHUNKS = 2
PC = FOCAL // CHUNKS
PG = PC // 8
BEGIN = (0.0, 2.3, 32.5, 34.8)
ROWS = 8 * SAMPLES // 2

ARRIVALS = (
    ((0, 1), "fy", 2.6),
    ((0, -1), "by", 2.7),
    ((1, 0), "", 2.8),
    ((0, 2), "f", 7.6),
    ((0, -2), "by", 7.7),
    ((1, 1), "f", 9.4),
    ((0, 3), "f", 12.5),
    ((1, -1), "", 12.6),
    ((1, 2), "f", 15.2),
    ((0, 4), "y", 16.5),
    ((1, -2), "b", 17.0),
    ((0, -3), "", 17.1),
    ((1, 3), "", 19.6),
    ((1, 4), "", 22.3),
    ((1, -3), "", 22.5),
)
END = 22.7
SLOT = {where: number for number, (where, _, _) in enumerate(ARRIVALS)}


def after(where, send):
    column, distance = where
    if send == "y":
        return (1 - column, distance)
    return (column, distance + (1 if send == "f" else -1))


def split(table):
    high = table.astype(ml_dtypes.bfloat16)
    low = (table - high.astype(np.float64)).astype(ml_dtypes.bfloat16)
    return np.stack([high, low])


def transforms():
    sample = np.arange(SAMPLES // 2)
    angle = 2.0 * np.pi * ((sample[:, None] * sample[None, :]) % SAMPLES) / SAMPLES
    weight = np.where(sample == 0, 1.0, 2.0)[:, None]
    tables = (np.cos(angle), np.sin(angle))
    eye = np.eye(8)
    forth = np.stack([np.kron(table / (SAMPLES // 2), eye) for table in tables])
    back = np.stack([np.kron((weight * table).T, eye) for table in tables])
    return split(forth), split(back)


def dot(left, right):
    return lax.dot_general(left, right, (((1,), (0,)), ((), ())), preferred_element_type=F32)


def dot_t(left, right):
    return lax.dot_general(left, right, (((1,), (1,)), ((), ())), preferred_element_type=F32)


def kernel(
    refl_hbm, plus_hbm, direct_hbm, arrival_hbm, forth_hbm, back_hbm,
    minus, following,
    refl, direct, arrival, forth, back, gathered, send_up, got_up, send_back, got_back, sums,
    load_sems, plus_sems, gather_recv, gather_send, swap_recv, swap_send,
):
    me_f = lax.axis_index("freq")
    me_r = lax.axis_index("rcv")
    core = lax.rem(me_f, 2)
    z = lax.div(me_r, 2)
    high = lax.rem(me_r, 2)
    turn = 1 - 2 * core

    def place(column, distance):
        ring = lax.rem(z - turn * distance + 2 * RING, RING)
        return ring * 2 + (high if column == 0 else 1 - high)

    targets = {
        "f": (me_f, place(0, -1)),
        "b": (me_f, place(0, 1)),
        "y": (me_f, place(1, 0)),
    }

    loads = [
        pltpu.make_async_copy(source, target, load_sems.at[number])
        for number, (source, target) in enumerate(
            ((refl_hbm, refl), (direct_hbm, direct), (arrival_hbm, arrival), (forth_hbm, forth), (back_hbm, back))
        )
    ]

    def block_of(job, where):
        return gathered.at[job, place(*where)]

    own = [
        pltpu.make_async_copy(
            plus_hbm.at[:, :, pl.ds(chunk * PC, PC), :], block_of(chunk, (0, 0)), plus_sems.at[chunk]
        )
        for chunk in range(CHUNKS)
    ]
    for copy in own:
        copy.start()
    for copy in loads:
        copy.start()

    barrier = pltpu.get_barrier_semaphore()
    for target in targets.values():
        pl.semaphore_signal(barrier, inc=1, device_id=target, device_id_type=MESH)

    @pl.loop(1, GROUP)
    def _(step):
        pl.semaphore_signal(
            barrier, inc=1, device_id=(lax.rem(me_f + step, GROUP), me_r), device_id_type=MESH
        )

    pl.semaphore_wait(barrier, 3 + GROUP - 1)

    def gather_copy(job, where, send):
        block = block_of(job, where)
        return pltpu.make_async_remote_copy(
            src_ref=block,
            dst_ref=block,
            send_sem=gather_send.at[job],
            recv_sem=gather_recv.at[job, SLOT[after(where, send)]],
            device_id=targets[send],
            device_id_type=MESH,
        )

    def gather_start(job):
        for send in "fby":
            gather_copy(job, (0, 0), send).start()

    def gather_step(job, number):
        where, sends, _ = ARRIVALS[number]
        block = block_of(job, where)
        pltpu.make_async_remote_copy(
            src_ref=block,
            dst_ref=block,
            send_sem=gather_send.at[job],
            recv_sem=gather_recv.at[job, number],
            device_id=targets["f"],
            device_id_type=MESH,
        ).wait_recv()
        for send in sends:
            gather_copy(job, where, send).start()

    def gather_end(job):
        sent = gathered.at[job, pl.ds(0, GROUP - 1)]
        pltpu.make_async_remote_copy(
            src_ref=sent,
            dst_ref=sent,
            send_sem=gather_send.at[job],
            recv_sem=gather_recv.at[job, 0],
            device_id=targets["f"],
            device_id_type=MESH,
        ).wait_send()

    def accumulate(job, where):
        owner = place(*where)
        here = pl.ds(pl.multiple_of(owner * BLOCK, BLOCK), BLOCK)
        for freq in range(2):
            left = gathered[job, owner, :, freq].reshape(2 * PC, BLOCK)
            for comp in range(2):
                term = dot_t(left, refl[comp, freq, :, here])
                if where == (0, 0):
                    sums[job % CHUNKS, freq, comp] = term
                else:
                    sums[job % CHUNKS, freq, comp] += term

    def products(job):
        parts = ([], [])
        for freq in range(2):
            with_real = sums[job % CHUNKS, freq, 0]
            with_imag = sums[job % CHUNKS, freq, 1]
            if job < CHUNKS:
                both = (with_real[:PC] - with_imag[PC:], with_real[PC:] + with_imag[:PC])
            else:
                both = (with_real[:PC] + with_imag[PC:], with_real[PC:] - with_imag[:PC])
            for comp in range(2):
                parts[comp].append(both[comp].reshape(PG, 8, BLOCK))
        for comp in range(2):
            send_up[job, pl.ds(comp * PG, PG)] = jnp.concatenate(parts[comp], axis=1).astype(BF)

    def swap_copy(job, way, sent, got, owner, count=1):
        if count == 1:
            source, target = sent.at[job, owner], got.at[job, me_f]
        else:
            source, target = sent.at[job, pl.ds(0, count)], got.at[job, pl.ds(0, count)]
        return pltpu.make_async_remote_copy(
            src_ref=source,
            dst_ref=target,
            send_sem=swap_send.at[job, way],
            recv_sem=swap_recv.at[job, way],
            device_id=(owner, me_r),
            device_id_type=MESH,
        )

    def swap_start(job, way, sent, got):
        for step in FAR_FIRST:
            swap_copy(job, way, sent, got, lax.rem(me_f + step, GROUP)).start()

        got[job, me_f] = sent[job, me_f]

    def swap_wait(job, way, sent, got):
        other = lax.rem(me_f + 1, GROUP)
        swap_copy(job, way, sent, got, other, GROUP - 1).wait_recv()

    def swap_end(job, way, sent, got):
        other = lax.rem(me_f + 1, GROUP)
        swap_copy(job, way, sent, got, other, GROUP - 1).wait_send()

    def window(job):
        comp = lax.div(me_f, PG)
        first = pl.multiple_of((job % CHUNKS) * PC + lax.rem(me_f, PG) * 8, 8)
        times = arrival[pl.ds(first, 8), :][None]
        spectra = got_up[job].reshape(ROWS, BLOCK)
        traces = dot(forth[0, comp], spectra) + dot(forth[1, comp], spectra)
        sample = lax.broadcasted_iota(jnp.int32, (SAMPLES // 2, 8, BLOCK), 0)
        kept = jnp.where(sample < times, traces.reshape(SAMPLES // 2, 8, BLOCK), 0.0).reshape(ROWS, BLOCK)
        upper = kept.astype(BF)
        lower = (kept - upper.astype(F32)).astype(BF)
        spectrum = dot(back[0, comp], upper) + dot(back[1, comp], upper) + dot(back[0, comp], lower)
        send_back[job] = spectrum.astype(BF).reshape(GROUP, 16, BLOCK)

    def returned(job):
        for comp in range(2):
            value = got_back[job, pl.ds(comp * PG, PG)].astype(F32)
            for freq in range(2):
                yield comp, freq, value[:, freq * 8:(freq + 1) * 8].reshape(PC, BLOCK)

    def place_minus(job):
        chunk = job % CHUNKS
        for comp, freq, value in returned(job):
            value = value.astype(BF)
            gathered[CHUNKS + chunk, me_r, comp, freq] = value
            minus[comp, freq, pl.ds(chunk * PC, PC), :] = value

    def place_next(job):
        chunk = job % CHUNKS
        here = pl.ds(chunk * PC, PC)
        for comp, freq, value in returned(job):
            value = value.astype(BF).astype(F32)
            following[comp, freq, here, :] = (direct[comp, freq, here, :].astype(F32) + value).astype(BF)

    steps = []

    def plan(when, what, *given):
        steps.append((when, functools.partial(what, *given)))

    def wait_all(*copies):
        for copy in copies:
            copy.wait()

    for job, begin in enumerate(BEGIN):
        if job < CHUNKS:
            plan(begin - 0.01, wait_all, own[job])
        plan(begin, gather_start, job)
        if job == 0:
            plan(begin + 0.5, wait_all, loads[0])
        plan(begin + 0.6, accumulate, job, (0, 0))
        for number, (where, _, due) in enumerate(ARRIVALS):
            plan(begin + due, gather_step, job, number)
            plan(begin + due + 0.05, accumulate, job, where)
        end = begin + END
        if job == 0:
            plan(end + 4.0, wait_all, *loads[2:])
        if job == CHUNKS:
            plan(end, wait_all, loads[1])
        plan(end, products, job)
        plan(end + 0.1, swap_start, job, 0, send_up, got_up)
        plan(end + 4.0, swap_wait, job, 0, send_up, got_up)
        plan(end + 4.1, window, job)
        plan(end + 4.2, swap_start, job, 1, send_back, got_back)
        plan(end + 8.5, swap_wait, job, 1, send_back, got_back)
        plan(end + 8.6, place_minus if job < CHUNKS else place_next, job)
    for _, step in sorted(steps, key=lambda entry: entry[0]):
        step()

    for job in range(2 * CHUNKS):
        gather_end(job)
        swap_end(job, 0, send_up, got_up)
        swap_end(job, 1, send_back, got_back)


def local(reflection, focus_plus, focus_direct, arrival):
    forth, back = transforms()
    jobs = 2 * CHUNKS
    swap = (jobs, GROUP, 16, BLOCK)
    in_vmem = pl.BlockSpec(memory_space=pltpu.VMEM)
    return pl.pallas_call(
        kernel,
        out_shape=(pltpu.VMEM(focus_plus.shape, BF),) * 2,
        in_specs=[pl.BlockSpec(memory_space=pl.ANY)] * 6,
        out_specs=(in_vmem, in_vmem),
        scratch_shapes=[
            pltpu.VMEM(reflection.shape, BF),
            pltpu.VMEM(focus_direct.shape, BF),
            pltpu.VMEM(arrival.shape, jnp.int32),
            pltpu.VMEM(forth.shape, BF),
            pltpu.VMEM(back.shape, BF),
            pltpu.VMEM((jobs, GROUP, 2, 2, PC, BLOCK), BF),
            pltpu.VMEM(swap, BF),
            pltpu.VMEM(swap, BF),
            pltpu.VMEM(swap, BF),
            pltpu.VMEM(swap, BF),
            pltpu.VMEM((CHUNKS, 2, 2, 2 * PC, BLOCK), F32),
            pltpu.SemaphoreType.DMA((5,)),
            pltpu.SemaphoreType.DMA((CHUNKS,)),
            pltpu.SemaphoreType.DMA((jobs, len(ARRIVALS))),
            pltpu.SemaphoreType.DMA((jobs,)),
            pltpu.SemaphoreType.DMA((jobs, 2)),
            pltpu.SemaphoreType.DMA((jobs, 2)),
        ],
        compiler_params=pltpu.CompilerParams(
            collective_id=0, has_side_effects=True, vmem_limit_bytes=62 * 2**20
        ),
    )(reflection, focus_plus, focus_direct, arrival, jnp.asarray(forth), jnp.asarray(back))


def solution(mesh):
    return jax.shard_map(
        local,
        mesh=mesh,
        in_specs=(
            P(None, "freq", "rcv", None),
            P(None, "freq", None, "rcv"),
            P(None, "freq", None, "rcv"),
            P(None, "rcv"),
        ),
        out_specs=(P(None, "freq", None, "rcv"), P(None, "freq", None, "rcv")),
        check_vma=False,
    )
```
